512 devices in a mesh: dp: 64 (over y_hi, z, core), tensor: 8 (over y_lo, x).
Axes of the slice: x: 4, y: 8 (y_hi: 4, y_lo: 2; y = y_hi * 2 + y_lo), z: 8, core: 2. Of those that a mesh axis runs over, the one named last changes fastest.
Arguments:
- activations: bfloat16 [40960, 2048], P('dp', 'tensor'), may hold values from -6 to 6
- cotangent: bfloat16 [40960, 2048], P('dp', 'tensor'), may hold values from -6 to 6
- kv_weight: bfloat16 [64, 2048, 2048], P('dp', None, 'tensor'), may hold values from -6 to 6
- momentum: bfloat16 [64, 2048, 2048], P('dp', None, 'tensor'), may hold values from -6 to 6
- alive_mask: int32 [64], P('dp'), may hold values 0 or 1
Outputs:
- new_weight: bfloat16 [64, 2048, 2048], P('dp', None, 'tensor')
- new_momentum: bfloat16 [64, 2048, 2048], P('dp', None, 'tensor')
- input_grad: bfloat16 [40960, 2048], P(('dp', 'tensor'))
The draws below stay inside these ranges and needn't reach their ends.
All inputs are finite; a program needn't handle non-finite values. No bound on the sum of `alive_mask` on one device may be relied on, other than what follows from the above.
Results may differ from the reference program's by a relative error of at most 0.017.
Values may be sent and summed in bfloat16 or wider, within the bound.
No kernel may reach another device: no remote copies, remote signals or barrier semaphores. Data moves between devices by JAX's collectives and lax.ppermute only.
A program may use at most 64 MiB of HBM per device.

```python
import math
import jax
import jax.numpy as jnp
from jax import lax

DW = 2048
KV_HEADS = 8
HEAD = 128
GROUP = 8
ROWS = 640
KV_WIDTH = 2048
TOKENS = 40960
N_DP = 64
N_TENSOR = 8


def with_ends(drawn, key, least, high):
    dims = drawn.shape
    spot = [jax.random.randint(jax.random.fold_in(key, axis), (), 0, dims[axis]) for axis in range(len(dims))]
    drawn = drawn.at[tuple(spot)].set(least)
    longest = dims.index(max(dims))
    spot[longest] = (spot[longest] + 1) % dims[longest]
    return drawn.at[tuple(spot)].set(high)


def levels(own_key, dims, split, low, high):
    def one(dim, blocks):
        draws = jax.random.uniform(jax.random.fold_in(jax.random.fold_in(own_key, 6), dim), (blocks,), jnp.float32, low / len(split), high / len(split))
        return jnp.repeat(jnp.exp(draws), dims[dim] // blocks).reshape((-1,) + (1,) * (len(dims) - dim - 1))

    level = one(*split[0])
    for cut in split[1:]:
        level = level * one(*cut)
    return level


def gaussian(key, shape, scale, reach, cuts=(), kind=jnp.bfloat16):
    entries = jax.random.normal(key, shape, jnp.float32) * scale
    if len(cuts) > 0:
        entries = levels(key, shape, cuts, -0.22, 0.18) * entries
    return jnp.clip(entries, min=-reach, max=reach).astype(kind)


def setup_inputs(seed: int = 0) -> dict:
    seeds = jax.random.split(jax.random.key(seed), 6)
    activations = gaussian(seeds[0], (TOKENS, DW), 1.0, 6.0, ((0, 64), (1, 8)))
    cotangent = gaussian(seeds[1], (TOKENS, KV_WIDTH), 1.0, 6.0, ((0, 64), (1, 8)))
    kv_weight = gaussian(seeds[2], (N_DP, DW, KV_WIDTH), 1.0, 6.0, ((0, 64), (2, 8)))
    momentum = gaussian(seeds[3], (N_DP, DW, KV_WIDTH), 1.0, 6.0, ((0, 64), (2, 8)))
    alive_mask = with_ends((jax.random.randint(seeds[4], (N_DP,), 0, 4) < 3).astype(jnp.int32), jax.random.fold_in(seeds[4], 1), 0, 1)
    return {"activations": activations, "cotangent": cotangent, "kv_weight": kv_weight, "momentum": momentum, "alive_mask": alive_mask}


step_size = 0.25
decay_factor = 0.9

def reference(activations, cotangent, kv_weight, momentum, alive_mask):
    unit_scale = 1.0 / math.sqrt(DW)
    kv_width = 2 * KV_HEADS * HEAD
    head_block = kv_width // N_TENSOR
    act_rows = activations.reshape(N_DP, ROWS, DW)
    cot_rows = cotangent.reshape(N_DP, ROWS, kv_width)
    live_flag = alive_mask.astype(jnp.float32)

    def update(one_replica):
        act_block, cot_block, weight, moment_old = one_replica
        gradient = lax.dot_general(act_block, cot_block, (((0,), (0,)), ((), ())), preferred_element_type=jnp.float32) * unit_scale
        moment_new = decay_factor * moment_old.astype(jnp.float32) + gradient
        weight_new = weight.astype(jnp.float32) - step_size * moment_new
        partials = jnp.zeros((ROWS, DW), jnp.float32)
        for member in range(N_TENSOR):
            cot_part = cot_block[:, member * head_block:(member + 1) * head_block]
            weight_part = weight[:, member * head_block:(member + 1) * head_block]
            term = jnp.dot(cot_part, weight_part.T, preferred_element_type=jnp.float32) * unit_scale
            rounded = lax.optimization_barrier(term.astype(jnp.bfloat16))
            partials = partials + rounded.astype(jnp.float32)
        return (weight_new, moment_new.astype(jnp.bfloat16), partials.astype(jnp.bfloat16))
    weights_new, moments_new, grad_rows = lax.map(update, (act_rows, cot_rows, kv_weight, momentum))
    group_count = N_DP // GROUP
    grouped = weights_new.reshape(group_count, GROUP, DW, kv_width)
    live_group = live_flag.reshape(group_count, GROUP)
    group_total = jnp.einsum('gr,grij->gij', live_group, grouped, precision=lax.Precision.HIGHEST)
    live_count = jnp.maximum(lax.optimization_barrier(jnp.sum(live_group, axis=1)), 1.0)
    average = group_total / live_count[:, None, None]
    averaged = jnp.where(live_group[:, :, None, None] > 0.5, average[:, None], grouped)
    new_weight = averaged.reshape(N_DP, DW, kv_width).astype(jnp.bfloat16)
    input_grad = grad_rows.reshape(N_DP * ROWS, DW)
    return (new_weight, moments_new, input_grad)
```

```python
import functools
import math

import jax
import jax.numpy as jnp
from jax import lax
from jax.experimental import pallas as pl
from jax.experimental.pallas import tpu as pltpu
from jax.sharding import PartitionSpec as P

GROUP = 8
step_size = 0.25
decay_factor = 0.9
bf16 = jnp.bfloat16
f32 = jnp.float32

EARLY = (0, 4, 1, 3)
LATE = (7, 5, 2, 6)
PAD = 16
VMEM = pl.BlockSpec(memory_space=pltpu.VMEM)
ANY = pl.BlockSpec(memory_space=pl.ANY)
SMEM = pl.BlockSpec(memory_space=pltpu.SMEM)
PARAMS = pltpu.CompilerParams(vmem_limit_bytes=16 * 1024 * 1024)


def tensor_swap(value, k):
    return lax.ppermute(value, "tensor", [(t, t ^ k) for t in range(lax.axis_size("tensor"))])


def core_swap(value):
    return lax.ppermute(value, "dp", [(r, r ^ 1) for r in range(lax.axis_size("dp"))])


def chip_exchange(value):
    groups = [
        [g * GROUP + 2 * z + c for z in range(GROUP // 2)]
        for g in range(lax.axis_size("dp") // GROUP)
        for c in range(2)
    ]
    return lax.all_to_all(value, "dp", 0, 0, axis_index_groups=groups, tiled=True)


def update_kernel(scale, first, info, *refs):
    n = 4
    acts, (cot, weight, mom) = refs[:n], refs[n : n + 3]
    if first:
        mom_out, own, keep, send = refs[n + 3 : n + 7]
    else:
        mom_out, own, keep, send = refs[n + 4 : n + 8]
    w_buf, m_buf, o_buf, sems = refs[-4:]
    size = w_buf.shape[1]

    def rows(b):
        return pl.ds(pl.multiple_of(info[b] * size, size), size)

    def loads(b):
        return (
            pltpu.make_async_copy(weight.at[rows(b)], w_buf.at[b], sems.at[0, b]),
            pltpu.make_async_copy(mom.at[rows(b)], m_buf.at[b], sems.at[1, b]),
        )

    def store(b):
        return pltpu.make_async_copy(o_buf.at[b], mom_out.at[rows(b)], sems.at[2, b])

    for b in range(n):
        for copy in loads(b):
            copy.start()
    core, alive = info[n], info[n + 1]
    flag = jnp.where(alive > 0, 1.0, 0.0).astype(f32)
    cot_value = cot[...]
    for b in range(n):
        grad = lax.dot_general(
            acts[b][...], cot_value, (((0,), (0,)), ((), ())), preferred_element_type=f32
        )
        for copy in loads(b):
            copy.wait()
        moment = decay_factor * m_buf[b].astype(f32) + grad * scale
        o_buf[b] = moment.astype(bf16)
        store(b).start()
        new = w_buf[b].astype(f32) - step_size * moment
        own[b] = new.astype(bf16)
        part = (new * flag).astype(bf16)
        place = pl.ds((b % 2) * size, size)

        @pl.when(core == b // 2)
        def _():
            keep[place, :] = part

        @pl.when(core != b // 2)
        def _():
            send[place, :] = part

    if first:
        tail = pl.ds(2 * size, PAD)
        keep[tail, :] = jnp.full((PAD, keep.shape[1]), flag, f32).astype(bf16)
        send[tail, :] = jnp.full((PAD, keep.shape[1]), flag, f32).astype(bf16)
    for b in range(n):
        store(b).wait()


def update(scale, info, acts, cot, weight, mom, mom_out):
    first = mom_out is None
    width = cot.shape[1]
    size = acts[0].shape[1]
    half = 2 * size + (PAD if first else 0)
    extra = () if first else (mom_out,)
    return pl.pallas_call(
        functools.partial(update_kernel, scale, first),
        out_shape=(
            jax.ShapeDtypeStruct(weight.shape, bf16),
            jax.ShapeDtypeStruct((4, size, width), bf16),
            jax.ShapeDtypeStruct((half, width), bf16),
            jax.ShapeDtypeStruct((half, width), bf16),
        ),
        in_specs=[SMEM] + [VMEM] * 5 + [ANY] * (2 + len(extra)),
        out_specs=(ANY, VMEM, VMEM, VMEM),
        scratch_shapes=[
            pltpu.VMEM((4, size, width), bf16),
            pltpu.VMEM((4, size, width), bf16),
            pltpu.VMEM((4, size, width), bf16),
            pltpu.SemaphoreType.DMA((3, 4)),
        ],
        input_output_aliases={} if first else {8: 0},
        compiler_params=PARAMS,
        cost_estimate=pl.CostEstimate(
            flops=2 * 4 * cot.shape[0] * size * width, bytes_accessed=4_000_000, transcendentals=0
        ),
    )(info, *acts, cot, weight, mom, *extra)


def place_kernel(info, *refs):
    ins, out, sems = refs[:6], refs[6], refs[7]
    size = ins[0].shape[1]
    core, alive = info[8], info[9]

    def copy(source, b):
        return pltpu.make_async_copy(
            source, out.at[pl.ds(pl.multiple_of(info[b] * size, size), size)], sems.at[b]
        )

    for b in range(8):
        own, mine, other = ins[3 * (b // 4) : 3 * (b // 4) + 3]
        at = pl.ds((b % 2) * size, size)
        is_mine = core == (b % 4) // 2

        @pl.when(alive <= 0)
        def _():
            copy(own.at[b % 4], b).start()

        @pl.when((alive > 0) & is_mine)
        def _():
            copy(mine.at[at], b).start()

        @pl.when((alive > 0) & jnp.logical_not(is_mine))
        def _():
            copy(other.at[at], b).start()

    for b in range(8):
        copy(ins[0].at[0], b).wait()


def place(info, parts, shape):
    return pl.pallas_call(
        place_kernel,
        out_shape=jax.ShapeDtypeStruct(shape, bf16),
        in_specs=[SMEM] + [VMEM] * 6,
        out_specs=ANY,
        scratch_shapes=[pltpu.SemaphoreType.DMA((8,))],
        compiler_params=PARAMS,
        cost_estimate=pl.CostEstimate(flops=0, bytes_accessed=2_000_000, transcendentals=0),
    )(info, *parts)


def body(activations, cotangent, kv_weight, momentum, alive_mask):
    weight, mom = kv_weight[0], momentum[0]
    features, width = weight.shape
    scale = 1.0 / math.sqrt(features)
    t = lax.axis_index("tensor")
    core = lax.rem(lax.axis_index("dp"), 2)
    alive = alive_mask[0]
    tail = jnp.stack([core, alive])
    early = jnp.stack([t ^ k for k in EARLY])
    late = jnp.stack([t ^ k for k in LATE])

    a_y = tensor_swap(activations, 4)
    a_p = tensor_swap(activations, 1)
    a_q = tensor_swap(activations, 3)
    a_qy = tensor_swap(a_y, 3)
    a_yp = tensor_swap(a_p, 4)
    a_pq = tensor_swap(a_q, 1)
    a_ypq = tensor_swap(a_pq, 4)

    partial = (
        lax.dot_general(cotangent, weight, (((1,), (1,)), ((), ())), preferred_element_type=f32)
        * scale
    ).astype(bf16)

    mom_1, own_1, keep_1, send_1 = update(
        scale, jnp.concatenate([early, tail]), (activations, a_y, a_p, a_q), cotangent, weight, mom, None
    )
    half = keep_1.shape[0] - PAD
    quarter = half // 4
    sum_1 = keep_1.astype(f32) + core_swap(send_1).astype(f32)
    flags = jnp.broadcast_to(sum_1[None, half:], (4, PAD, width))
    out_1 = jnp.concatenate([sum_1[:half].reshape(4, quarter, width), flags], axis=1).astype(bf16)
    got_1 = chip_exchange(out_1).astype(f32).sum(0)
    count = jnp.maximum(got_1[quarter : quarter + 1, :1], 1.0)
    mean_1 = (got_1[:quarter] / count).astype(bf16)

    new_momentum, own_2, keep_2, send_2 = update(
        scale, jnp.concatenate([late, tail]), (a_qy, a_yp, a_pq, a_ypq), cotangent, weight, mom, mom_1
    )
    sum_2 = keep_2.astype(f32) + core_swap(send_2).astype(f32)
    got_2 = chip_exchange(sum_2.astype(bf16).reshape(4, quarter, width)).astype(f32).sum(0)
    mean_2 = (got_2 / count).astype(bf16)

    mine_1 = chip_exchange(jnp.broadcast_to(mean_1[None], (4, quarter, width))).reshape(half, width)
    other_1 = core_swap(mine_1)
    mine_2 = chip_exchange(jnp.broadcast_to(mean_2[None], (4, quarter, width))).reshape(half, width)
    other_2 = core_swap(mine_2)

    new_weight = place(
        jnp.concatenate([early, late, tail]),
        (own_1, mine_1, other_1, own_2, mine_2, other_2),
        weight.shape,
    )

    members = lax.axis_size("tensor")
    partial, _ = lax.optimization_barrier((partial, own_2))
    parts = lax.all_to_all(
        partial.reshape(members, partial.shape[0] // members, features), "tensor", 0, 0, tiled=True
    )
    input_grad = parts.astype(f32).sum(0).astype(bf16)
    return new_weight[None], new_momentum[None], input_grad


def solution(mesh):
    return jax.shard_map(
        body,
        mesh=mesh,
        in_specs=(
            P("dp", "tensor"),
            P("dp", "tensor"),
            P("dp", None, "tensor"),
            P("dp", None, "tensor"),
            P("dp"),
        ),
        out_specs=(P("dp", None, "tensor"), P("dp", None, "tensor"), P(("dp", "tensor"), None)),
        check_vma=False,
    )
```

```python
import functools
import math

import jax
import jax.numpy as jnp
from jax import lax
from jax.experimental import pallas as pl
from jax.experimental.pallas import tpu as pltpu
from jax.sharding import PartitionSpec as P

GROUP = 8
step_size = 0.25
decay_factor = 0.9
bf16 = jnp.bfloat16
f32 = jnp.float32

EARLY = (0, 4, 1, 3)
LATE = (5, 2, 7, 6)
PAD = 16
VMEM = pl.BlockSpec(memory_space=pltpu.VMEM)
ANY = pl.BlockSpec(memory_space=pl.ANY)
SMEM = pl.BlockSpec(memory_space=pltpu.SMEM)
PARAMS = pltpu.CompilerParams(vmem_limit_bytes=56 * 1024 * 1024)
CHEAP = pl.CostEstimate(flops=1000, bytes_accessed=1000, transcendentals=0)


def tensor_swap(value, k):
    return lax.ppermute(value, "tensor", [(t, t ^ k) for t in range(lax.axis_size("tensor"))])


def core_swap(value):
    return lax.ppermute(value, "dp", [(r, r ^ 1) for r in range(lax.axis_size("dp"))])


def chip_swap(value, k):
    return lax.ppermute(value, "dp", [(r, r ^ (2 * k)) for r in range(lax.axis_size("dp"))])


def after(value, *earlier):
    return lax.optimization_barrier((value, *earlier))[0]


def update_kernel(scale, first, info, *refs):
    n = 4
    acts, (cot, weight, mom) = refs[:n], refs[n : n + 3]
    mom_out, keep, send, own = refs[n + 3 : n + 7] if first else refs[n + 6 : n + 10]
    a_buf, c_buf, w_buf, m_buf, o_buf, n_buf, p_buf, f_buf, sems = refs[-9:]
    size = w_buf.shape[1]
    width = w_buf.shape[2]
    core, chip, alive = info[n], info[n + 1], info[n + 2]

    def rows(b):
        return pl.ds(pl.multiple_of(info[b] * size, size), size)

    def loads(b):
        return (
            pltpu.make_async_copy(acts[b], a_buf.at[b], sems.at[0, b]),
            pltpu.make_async_copy(weight.at[rows(b)], w_buf.at[b], sems.at[1, b]),
            pltpu.make_async_copy(mom.at[rows(b)], m_buf.at[b], sems.at[2, b]),
        )

    def stores(b):
        return (
            pltpu.make_async_copy(o_buf.at[b], mom_out.at[rows(b)], sems.at[3, b]),
            pltpu.make_async_copy(n_buf.at[b], own.at[b], sems.at[4, b]),
        )

    def hand_over(b, target):
        place = (b % 2 + (0 if first else 2)) ^ chip
        return pltpu.make_async_copy(
            p_buf.at[b], target.at[place, pl.ds(0, size)], sems.at[5, b]
        )

    def flags(k):
        return tuple(
            pltpu.make_async_copy(f_buf, target.at[k, pl.ds(size, PAD)], sems.at[6 + i, k])
            for i, target in enumerate((keep, send))
        )

    load_cot = pltpu.make_async_copy(cot, c_buf, sems.at[8, 0])
    load_cot.start()
    for b in range(n):
        for copy in loads(b):
            copy.start()
    flag = jnp.where(alive > 0, 1.0, 0.0).astype(f32)
    if first:
        f_buf[...] = jnp.full((PAD, width), flag, f32).astype(bf16)
        for k in range(4):
            for copy in flags(k):
                copy.start()
    load_cot.wait()
    for b in range(n):
        for copy in loads(b):
            copy.wait()
        grad = lax.dot_general(
            a_buf[b], c_buf[...], (((0,), (0,)), ((), ())), preferred_element_type=f32
        )
        moment = decay_factor * m_buf[b].astype(f32) + grad * scale
        o_buf[b] = moment.astype(bf16)
        new = w_buf[b].astype(f32) - step_size * moment
        n_buf[b] = new.astype(bf16)
        p_buf[b] = (new * flag).astype(bf16)
        for copy in stores(b):
            copy.start()

        @pl.when(core == b // 2)
        def _():
            hand_over(b, keep).start()

        @pl.when(core != b // 2)
        def _():
            hand_over(b, send).start()

    for b in range(n):
        for copy in stores(b):
            copy.wait()
        hand_over(b, keep).wait()
    if first:
        for k in range(4):
            for copy in flags(k):
                copy.wait()


def update(scale, info, acts, cot, weight, mom, done=()):
    first = not done
    rows, size = acts[0].shape
    width = cot.shape[1]
    block = pltpu.VMEM((4, size, width), bf16)
    return pl.pallas_call(
        functools.partial(update_kernel, scale, first),
        out_shape=(
            jax.ShapeDtypeStruct(weight.shape, bf16),
            jax.ShapeDtypeStruct((4, size + PAD, width), bf16),
            jax.ShapeDtypeStruct((4, size + PAD, width), bf16),
            jax.ShapeDtypeStruct((4, size, width), bf16),
        ),
        in_specs=[SMEM] + [ANY] * (7 + len(done)),
        out_specs=(ANY, ANY, ANY, ANY),
        scratch_shapes=[
            pltpu.VMEM((4, rows, size), bf16),
            pltpu.VMEM((rows, width), bf16),
            block,
            block,
            block,
            block,
            block,
            pltpu.VMEM((PAD, width), bf16),
            pltpu.SemaphoreType.DMA((9, 4)),
        ],
        input_output_aliases={} if first else {8: 0, 9: 1, 10: 2},
        compiler_params=PARAMS,
        cost_estimate=CHEAP,
    )(info, *acts, cot, weight, mom, *done)


def partial_kernel(scale, cot, weight, out, c_buf, w_buf, buf, sems):
    tiles = 4
    size = weight.shape[0] // tiles

    def load(n):
        at = pl.ds(n * size, size)
        return pltpu.make_async_copy(weight.at[at], w_buf.at[at], sems.at[n])

    def store(n):
        return pltpu.make_async_copy(buf.at[n], out.at[:, pl.ds(n * size, size)], sems.at[tiles + n])

    load_cot = pltpu.make_async_copy(cot, c_buf, sems.at[2 * tiles])
    load_cot.start()
    for n in range(tiles):
        load(n).start()
    load_cot.wait()
    for n in range(tiles):
        load(n).wait()
        value = lax.dot_general(
            c_buf[...],
            w_buf[n * size : (n + 1) * size, :],
            (((1,), (1,)), ((), ())),
            preferred_element_type=f32,
        )
        buf[n] = (value * scale).astype(bf16)
        store(n).start()
    for n in range(tiles):
        store(n).wait()


def partials(scale, cot, weight):
    rows, features = cot.shape[0], weight.shape[0]
    return pl.pallas_call(
        functools.partial(partial_kernel, scale),
        out_shape=jax.ShapeDtypeStruct((rows, features), bf16),
        in_specs=[ANY, ANY],
        out_specs=ANY,
        scratch_shapes=[
            pltpu.VMEM(cot.shape, bf16),
            pltpu.VMEM(weight.shape, bf16),
            pltpu.VMEM((4, rows, features // 4), bf16),
            pltpu.SemaphoreType.DMA((9,)),
        ],
        compiler_params=PARAMS,
        cost_estimate=CHEAP,
    )(cot, weight)


def place_kernel(info, own_1, own_2, mine, other, out, sems):
    size = mine.shape[1]
    core, chip, alive = info[8], info[9], info[10]

    def copy(source, b):
        at = pl.ds(pl.multiple_of(info[b] * size, size), size)
        return pltpu.make_async_copy(source, out.at[at], sems.at[b])

    for b in range(8):
        own = own_1 if b < 4 else own_2
        slot = (b % 2 + 2 * (b // 4)) ^ chip
        is_mine = core == (b % 4) // 2

        @pl.when(alive <= 0)
        def _():
            copy(own.at[b % 4], b).start()

        @pl.when((alive > 0) & is_mine)
        def _():
            copy(mine.at[slot], b).start()

        @pl.when((alive > 0) & jnp.logical_not(is_mine))
        def _():
            copy(other.at[slot], b).start()

    for b in range(8):
        copy(mine.at[0], b).wait()


def place(info, parts, shape):
    return pl.pallas_call(
        place_kernel,
        out_shape=jax.ShapeDtypeStruct(shape, bf16),
        in_specs=[SMEM] + [VMEM] * 4,
        out_specs=ANY,
        scratch_shapes=[pltpu.SemaphoreType.DMA((8,))],
        compiler_params=PARAMS,
        cost_estimate=CHEAP,
    )(info, *parts)


def body(activations, cotangent, kv_weight, momentum, alive_mask):
    weight, mom = kv_weight[0], momentum[0]
    features, width = weight.shape
    scale = 1.0 / math.sqrt(features)
    t = lax.axis_index("tensor")
    core = lax.rem(lax.axis_index("dp"), 2)
    alive = alive_mask[0]
    chip = lax.rem(lax.axis_index("dp") // 2, GROUP // 2)
    tail = jnp.stack([core, chip, alive])
    early = jnp.stack([t ^ k for k in EARLY])
    late = jnp.stack([t ^ k for k in LATE])

    a_y = tensor_swap(activations, 4)
    a_p = tensor_swap(activations, 1)
    a_q = tensor_swap(activations, 3)
    share = partials(scale, cotangent, weight)
    a_y, a_p, a_q, share = lax.optimization_barrier((a_y, a_p, a_q, share))

    a_yp = tensor_swap(a_p, 4)
    a_pq = tensor_swap(a_q, 1)
    a_qy = tensor_swap(a_y, 3)
    a_ypq = tensor_swap(after(activations, a_q), 6)
    *done, own_1 = update(
        scale,
        jnp.concatenate([early, tail]),
        (activations, a_y, a_p, a_q),
        cotangent,
        weight,
        mom,
    )
    a_yp, a_pq, a_qy, a_ypq, share, *done = lax.optimization_barrier(
        (a_yp, a_pq, a_qy, a_ypq, share, *done)
    )
    new_momentum, keep, send, own_2 = update(
        scale, jnp.concatenate([late, tail]), (a_yp, a_pq, a_qy, a_ypq), cotangent, weight, mom, done
    )

    members = lax.axis_size("tensor")
    share = after(share, send)
    shares = lax.all_to_all(
        share.reshape(members, share.shape[0] // members, features), "tensor", 0, 0, tiled=True
    )

    arrived = core_swap(send)
    sums = [(keep[k].astype(f32) + arrived[k].astype(f32)).astype(bf16) for k in range(4)]
    size = sums[0].shape[0] - PAD
    got = sums[0].astype(f32)
    for k in (1, 2, 3):
        got = got + chip_swap(sums[k], k).astype(f32)
    count = jnp.maximum(got[size : size + 1], 1.0)
    mean = (got[:size] / count).astype(bf16)
    mine = jnp.stack([mean] + [chip_swap(mean, k) for k in (1, 2, 3)])
    other = core_swap(mine)
    new_weight = place(jnp.concatenate([early, late, tail]), (own_1, own_2, mine, other), weight.shape)
    input_grad = shares.astype(f32).sum(0).astype(bf16)
    return new_weight[None], new_momentum[None], input_grad


def solution(mesh):
    return jax.shard_map(
        body,
        mesh=mesh,
        in_specs=(
            P("dp", "tensor"),
            P("dp", "tensor"),
            P("dp", None, "tensor"),
            P("dp", None, "tensor"),
            P("dp"),
        ),
        out_specs=(P("dp", None, "tensor"), P("dp", None, "tensor"), P(("dp", "tensor"), None)),
        check_vma=False,
    )
```

```python
import functools
import math

import jax
import jax.numpy as jnp
from jax import lax
from jax.experimental import pallas as pl
from jax.experimental.pallas import tpu as pltpu
from jax.sharding import PartitionSpec as P

GROUP = 8
step_size = 0.25
decay_factor = 0.9
bf16 = jnp.bfloat16
f32 = jnp.float32

EARLY = (0, 4, 1, 3)
LATE = (5, 2, 7, 6)
PAD = 16
VMEM = pl.BlockSpec(memory_space=pltpu.VMEM)
ANY = pl.BlockSpec(memory_space=pl.ANY)
SMEM = pl.BlockSpec(memory_space=pltpu.SMEM)
PARAMS = pltpu.CompilerParams(vmem_limit_bytes=56 * 1024 * 1024)
CHEAP = pl.CostEstimate(flops=1000, bytes_accessed=1000, transcendentals=0)


def tensor_swap(value, k):
    return lax.ppermute(value, "tensor", [(t, t ^ k) for t in range(lax.axis_size("tensor"))])


def core_swap(value):
    return lax.ppermute(value, "dp", [(r, r ^ 1) for r in range(lax.axis_size("dp"))])


def chip_swap(value, k):
    return lax.ppermute(value, "dp", [(r, r ^ (2 * k)) for r in range(lax.axis_size("dp"))])


def after(value, *earlier):
    return lax.optimization_barrier((value, *earlier))[0]


def update_kernel(scale, first, info, *refs):
    n = 4
    base = 0 if first else n
    acts, (cot, weight, mom) = refs[:n], refs[n : n + 3]
    mom_out, keep, send, own = refs[n + 3 : n + 7] if first else refs[n + 6 : n + 10]
    a_buf, c_buf, w_buf, m_buf, o_buf, n_buf, p_buf, f_buf, sems = refs[-9:]
    size = w_buf.shape[1]
    width = w_buf.shape[2]
    core, chip, alive = info[8], info[9], info[10]

    def rows(b):
        return pl.ds(pl.multiple_of(info[base + b] * size, size), size)

    def loads(b):
        return (
            pltpu.make_async_copy(acts[b], a_buf.at[b], sems.at[0, b]),
            pltpu.make_async_copy(weight.at[rows(b)], w_buf.at[b], sems.at[1, b]),
            pltpu.make_async_copy(mom.at[rows(b)], m_buf.at[b], sems.at[2, b]),
        )

    def stores(b):
        return (
            pltpu.make_async_copy(o_buf.at[b], mom_out.at[rows(b)], sems.at[3, b]),
            pltpu.make_async_copy(n_buf.at[b], own.at[b], sems.at[4, b]),
        )

    def hand_over(b, target):
        place = (b % 2 + (0 if first else 2)) ^ chip
        return pltpu.make_async_copy(
            p_buf.at[b], target.at[place, pl.ds(0, size)], sems.at[5, b]
        )

    def flags(k):
        return tuple(
            pltpu.make_async_copy(f_buf, target.at[k, pl.ds(size, PAD)], sems.at[6 + i, k])
            for i, target in enumerate((keep, send))
        )

    load_cot = pltpu.make_async_copy(cot, c_buf, sems.at[8, 0])
    load_cot.start()
    for b in range(n):
        for copy in loads(b):
            copy.start()
    flag = jnp.where(alive > 0, 1.0, 0.0).astype(f32)
    if first:
        f_buf[...] = jnp.full((PAD, width), flag, f32).astype(bf16)
        for k in range(4):
            for copy in flags(k):
                copy.start()
    load_cot.wait()
    for b in range(n):
        for copy in loads(b):
            copy.wait()
        grad = lax.dot_general(
            a_buf[b], c_buf[...], (((0,), (0,)), ((), ())), preferred_element_type=f32
        )
        moment = decay_factor * m_buf[b].astype(f32) + grad * scale
        o_buf[b] = moment.astype(bf16)
        new = w_buf[b].astype(f32) - step_size * moment
        n_buf[b] = new.astype(bf16)
        p_buf[b] = (new * flag).astype(bf16)
        for copy in stores(b):
            copy.start()

        @pl.when(core == b // 2)
        def _():
            hand_over(b, keep).start()

        @pl.when(core != b // 2)
        def _():
            hand_over(b, send).start()

    for b in range(n):
        for copy in stores(b):
            copy.wait()
        hand_over(b, keep).wait()
    if first:
        for k in range(4):
            for copy in flags(k):
                copy.wait()


def update(scale, info, acts, cot, weight, mom, done=()):
    first = not done
    rows, size = acts[0].shape
    width = cot.shape[1]
    block = pltpu.VMEM((4, size, width), bf16)
    return pl.pallas_call(
        functools.partial(update_kernel, scale, first),
        out_shape=(
            jax.ShapeDtypeStruct(weight.shape, bf16),
            jax.ShapeDtypeStruct((4, size + PAD, width), bf16),
            jax.ShapeDtypeStruct((4, size + PAD, width), bf16),
            jax.ShapeDtypeStruct((4, size, width), bf16),
        ),
        in_specs=[SMEM] + [ANY] * (7 + len(done)),
        out_specs=(ANY, ANY, ANY, ANY),
        scratch_shapes=[
            pltpu.VMEM((4, rows, size), bf16),
            pltpu.VMEM((rows, width), bf16),
            block,
            block,
            block,
            block,
            block,
            pltpu.VMEM((PAD, width), bf16),
            pltpu.SemaphoreType.DMA((9, 4)),
        ],
        input_output_aliases={} if first else {8: 0, 9: 1, 10: 2},
        compiler_params=PARAMS,
        cost_estimate=CHEAP,
    )(info, *acts, cot, weight, mom, *done)


def partial_kernel(scale, cot, weight, out, c_buf, w_buf, buf, sems):
    tiles = 4
    size = weight.shape[0] // tiles

    def load(n):
        at = pl.ds(n * size, size)
        return pltpu.make_async_copy(weight.at[at], w_buf.at[at], sems.at[n])

    def store(n):
        return pltpu.make_async_copy(buf.at[n], out.at[:, pl.ds(n * size, size)], sems.at[tiles + n])

    load_cot = pltpu.make_async_copy(cot, c_buf, sems.at[2 * tiles])
    load_cot.start()
    for n in range(tiles):
        load(n).start()
    load_cot.wait()
    for n in range(tiles):
        load(n).wait()
        value = lax.dot_general(
            c_buf[...],
            w_buf[n * size : (n + 1) * size, :],
            (((1,), (1,)), ((), ())),
            preferred_element_type=f32,
        )
        buf[n] = (value * scale).astype(bf16)
        store(n).start()
    for n in range(tiles):
        store(n).wait()


def partials(scale, cot, weight):
    rows, features = cot.shape[0], weight.shape[0]
    return pl.pallas_call(
        functools.partial(partial_kernel, scale),
        out_shape=jax.ShapeDtypeStruct((rows, features), bf16),
        in_specs=[ANY, ANY],
        out_specs=ANY,
        scratch_shapes=[
            pltpu.VMEM(cot.shape, bf16),
            pltpu.VMEM(weight.shape, bf16),
            pltpu.VMEM((4, rows, features // 4), bf16),
            pltpu.SemaphoreType.DMA((9,)),
        ],
        compiler_params=PARAMS,
        cost_estimate=CHEAP,
    )(cot, weight)


def place_kernel(info, own_1, own_2, mine, other, out, sems):
    size = mine.shape[1]
    core, chip, alive = info[8], info[9], info[10]

    def copy(source, b):
        at = pl.ds(pl.multiple_of(info[b] * size, size), size)
        return pltpu.make_async_copy(source, out.at[at], sems.at[b])

    for b in range(8):
        own = own_1 if b < 4 else own_2
        slot = (b % 2 + 2 * (b // 4)) ^ chip
        is_mine = core == (b % 4) // 2

        @pl.when(alive <= 0)
        def _():
            copy(own.at[b % 4], b).start()

        @pl.when((alive > 0) & is_mine)
        def _():
            copy(mine.at[slot], b).start()

        @pl.when((alive > 0) & jnp.logical_not(is_mine))
        def _():
            copy(other.at[slot], b).start()

    for b in range(8):
        copy(mine.at[0], b).wait()


def place(info, parts, shape):
    return pl.pallas_call(
        place_kernel,
        out_shape=jax.ShapeDtypeStruct(shape, bf16),
        in_specs=[SMEM] + [VMEM] * 4,
        out_specs=ANY,
        scratch_shapes=[pltpu.SemaphoreType.DMA((8,))],
        compiler_params=PARAMS,
        cost_estimate=CHEAP,
    )(info, *parts)


def body(activations, cotangent, kv_weight, momentum, alive_mask):
    weight, mom = kv_weight[0], momentum[0]
    features, width = weight.shape
    scale = 1.0 / math.sqrt(features)
    t = lax.axis_index("tensor")
    core = lax.rem(lax.axis_index("dp"), 2)
    alive = alive_mask[0]
    chip = lax.rem(lax.axis_index("dp") // 2, GROUP // 2)
    info = jnp.stack([t ^ k for k in EARLY + LATE] + [core, chip, alive])

    a_y = tensor_swap(activations, 4)
    a_p = tensor_swap(activations, 1)
    a_q = tensor_swap(activations, 3)
    share = partials(scale, cotangent, weight)
    a_y, a_p, a_q, share = lax.optimization_barrier((a_y, a_p, a_q, share))

    a_yp = tensor_swap(a_p, 4)
    a_pq = tensor_swap(a_q, 1)
    a_qy = tensor_swap(a_y, 3)
    a_ypq = tensor_swap(after(activations, a_q), 6)
    *done, own_1 = update(
        scale,
        info,
        (activations, a_y, a_p, a_q),
        cotangent,
        weight,
        mom,
    )
    a_yp, a_pq, a_qy, a_ypq, share, *done = lax.optimization_barrier(
        (a_yp, a_pq, a_qy, a_ypq, share, *done)
    )
    new_momentum, keep, send, own_2 = update(
        scale, info, (a_yp, a_pq, a_qy, a_ypq), cotangent, weight, mom, done
    )

    members = lax.axis_size("tensor")
    share = after(share, send)
    shares = lax.all_to_all(
        share.reshape(members, share.shape[0] // members, features), "tensor", 0, 0, tiled=True
    )

    arrived = core_swap(send)
    sums = [(keep[k].astype(f32) + arrived[k].astype(f32)).astype(bf16) for k in range(4)]
    size = sums[0].shape[0] - PAD
    got = sums[0].astype(f32)
    for k in (3, 2, 1):
        got = got + chip_swap(sums[k], k).astype(f32)
    count = jnp.maximum(got[size : size + 1], 1.0)
    mean = (got[:size] / count).astype(bf16)
    mine = jnp.stack([mean] + [chip_swap(mean, k) for k in (1, 2, 3)])
    other = core_swap(mine)
    input_grad = shares.astype(f32).sum(0).astype(bf16)
    mine, input_grad = lax.optimization_barrier((mine, input_grad))
    new_weight = place(info, (own_1, own_2, mine, other), weight.shape)
    return new_weight[None], new_momentum[None], input_grad


def solution(mesh):
    return jax.shard_map(
        body,
        mesh=mesh,
        in_specs=(
            P("dp", "tensor"),
            P("dp", "tensor"),
            P("dp", None, "tensor"),
            P("dp", None, "tensor"),
            P("dp"),
        ),
        out_specs=(P("dp", None, "tensor"), P("dp", None, "tensor"), P(("dp", "tensor"), None)),
        check_vma=False,
    )
```

```python
import functools
import math

import jax
import jax.numpy as jnp
from jax import lax
from jax.experimental import pallas as pl
from jax.experimental.pallas import tpu as pltpu
from jax.sharding import PartitionSpec as P

GROUP = 8
step_size = 0.25
decay_factor = 0.9
bf16 = jnp.bfloat16
f32 = jnp.float32

EARLY = (0, 4, 1, 3)
LATE = (5, 2, 7, 6)
PAD = 16
VMEM = pl.BlockSpec(memory_space=pltpu.VMEM)
ANY = pl.BlockSpec(memory_space=pl.ANY)
SMEM = pl.BlockSpec(memory_space=pltpu.SMEM)
PARAMS = pltpu.CompilerParams(vmem_limit_bytes=56 * 1024 * 1024)
CHEAP = pl.CostEstimate(flops=1000, bytes_accessed=1000, transcendentals=0)


def tensor_swap(value, k):
    return lax.ppermute(value, "tensor", [(t, t ^ k) for t in range(lax.axis_size("tensor"))])


def core_swap(value):
    return lax.ppermute(value, "dp", [(r, r ^ 1) for r in range(lax.axis_size("dp"))])


def chip_swap(value, k):
    return lax.ppermute(value, "dp", [(r, r ^ (2 * k)) for r in range(lax.axis_size("dp"))])


def after(value, *earlier):
    return lax.optimization_barrier((value, *earlier))[0]


def update_kernel(scale, first, info, *refs):
    n = 4
    base = 0 if first else n
    acts, (cot, weight, mom) = refs[:n], refs[n : n + 3]
    mom_out, keep, send, own = refs[n + 3 : n + 7] if first else refs[n + 6 : n + 10]
    a_buf, c_buf, w_buf, m_buf, o_buf, n_buf, p_buf, f_buf, sems = refs[-9:]
    size = w_buf.shape[1]
    width = w_buf.shape[2]
    core, chip, alive = info[8], info[9], info[10]

    def rows(b):
        return pl.ds(pl.multiple_of(info[base + b] * size, size), size)

    def loads(b):
        return (
            pltpu.make_async_copy(acts[b], a_buf.at[b], sems.at[0, b]),
            pltpu.make_async_copy(weight.at[rows(b)], w_buf.at[b], sems.at[1, b]),
            pltpu.make_async_copy(mom.at[rows(b)], m_buf.at[b], sems.at[2, b]),
        )

    def stores(b):
        return (
            pltpu.make_async_copy(o_buf.at[b], mom_out.at[rows(b)], sems.at[3, b]),
            pltpu.make_async_copy(n_buf.at[b], own.at[b], sems.at[4, b]),
        )

    def hand_over(b, target):
        place = (b % 2 + (0 if first else 2)) ^ chip
        return pltpu.make_async_copy(
            p_buf.at[b], target.at[place, pl.ds(0, size)], sems.at[5, b]
        )

    def flags(k):
        return tuple(
            pltpu.make_async_copy(f_buf, target.at[k, pl.ds(size, PAD)], sems.at[6 + i, k])
            for i, target in enumerate((keep, send))
        )

    load_cot = pltpu.make_async_copy(cot, c_buf, sems.at[8, 0])
    load_cot.start()
    for b in range(n):
        for copy in loads(b):
            copy.start()
    flag = jnp.where(alive > 0, 1.0, 0.0).astype(f32)
    if first:
        f_buf[...] = jnp.full((PAD, width), flag, f32).astype(bf16)
        for k in range(4):
            for copy in flags(k):
                copy.start()
    load_cot.wait()
    for b in range(n):
        for copy in loads(b):
            copy.wait()
        grad = lax.dot_general(
            a_buf[b], c_buf[...], (((0,), (0,)), ((), ())), preferred_element_type=f32
        )
        moment = decay_factor * m_buf[b].astype(f32) + grad * scale
        o_buf[b] = moment.astype(bf16)
        new = w_buf[b].astype(f32) - step_size * moment
        n_buf[b] = new.astype(bf16)
        p_buf[b] = (new * flag).astype(bf16)
        for copy in stores(b):
            copy.start()

        @pl.when(core == b // 2)
        def _():
            hand_over(b, keep).start()

        @pl.when(core != b // 2)
        def _():
            hand_over(b, send).start()

    for b in range(n):
        for copy in stores(b):
            copy.wait()
        hand_over(b, keep).wait()
    if first:
        for k in range(4):
            for copy in flags(k):
                copy.wait()


def update(scale, info, acts, cot, weight, mom, done=()):
    first = not done
    rows, size = acts[0].shape
    width = cot.shape[1]
    block = pltpu.VMEM((4, size, width), bf16)
    return pl.pallas_call(
        functools.partial(update_kernel, scale, first),
        out_shape=(
            jax.ShapeDtypeStruct(weight.shape, bf16),
            jax.ShapeDtypeStruct((4, size + PAD, width), bf16),
            jax.ShapeDtypeStruct((4, size + PAD, width), bf16),
            jax.ShapeDtypeStruct((4, size, width), bf16),
        ),
        in_specs=[SMEM] + [ANY] * (7 + len(done)),
        out_specs=(ANY, ANY, ANY, ANY),
        scratch_shapes=[
            pltpu.VMEM((4, rows, size), bf16),
            pltpu.VMEM((rows, width), bf16),
            block,
            block,
            block,
            block,
            block,
            pltpu.VMEM((PAD, width), bf16),
            pltpu.SemaphoreType.DMA((9, 4)),
        ],
        input_output_aliases={} if first else {8: 0, 9: 1, 10: 2},
        compiler_params=PARAMS,
        cost_estimate=CHEAP,
    )(info, *acts, cot, weight, mom, *done)


def partial_kernel(scale, cot, weight, out, c_buf, w_buf, buf, sems):
    tiles = 4
    size = weight.shape[0] // tiles

    def load(n):
        at = pl.ds(n * size, size)
        return pltpu.make_async_copy(weight.at[at], w_buf.at[at], sems.at[n])

    def store(n):
        return pltpu.make_async_copy(buf.at[n], out.at[:, pl.ds(n * size, size)], sems.at[tiles + n])

    load_cot = pltpu.make_async_copy(cot, c_buf, sems.at[2 * tiles])
    load_cot.start()
    for n in range(tiles):
        load(n).start()
    load_cot.wait()
    for n in range(tiles):
        load(n).wait()
        value = lax.dot_general(
            c_buf[...],
            w_buf[n * size : (n + 1) * size, :],
            (((1,), (1,)), ((), ())),
            preferred_element_type=f32,
        )
        buf[n] = (value * scale).astype(bf16)
        store(n).start()
    for n in range(tiles):
        store(n).wait()


def partials(scale, cot, weight):
    rows, features = cot.shape[0], weight.shape[0]
    return pl.pallas_call(
        functools.partial(partial_kernel, scale),
        out_shape=jax.ShapeDtypeStruct((rows, features), bf16),
        in_specs=[ANY, ANY],
        out_specs=ANY,
        scratch_shapes=[
            pltpu.VMEM(cot.shape, bf16),
            pltpu.VMEM(weight.shape, bf16),
            pltpu.VMEM((4, rows, features // 4), bf16),
            pltpu.SemaphoreType.DMA((9,)),
        ],
        compiler_params=PARAMS,
        cost_estimate=CHEAP,
    )(cot, weight)


def place_kernel(info, own_1, own_2, mine, other, out, sems):
    size = mine.shape[1]
    core, chip, alive = info[8], info[9], info[10]

    def copy(source, b):
        at = pl.ds(pl.multiple_of(info[b] * size, size), size)
        return pltpu.make_async_copy(source, out.at[at], sems.at[b])

    for b in range(8):
        own = own_1 if b < 4 else own_2
        slot = (b % 2 + 2 * (b // 4)) ^ chip
        is_mine = core == (b % 4) // 2

        @pl.when(alive <= 0)
        def _():
            copy(own.at[b % 4], b).start()

        @pl.when((alive > 0) & is_mine)
        def _():
            copy(mine.at[slot], b).start()

        @pl.when((alive > 0) & jnp.logical_not(is_mine))
        def _():
            copy(other.at[slot], b).start()

    for b in range(8):
        copy(mine.at[0], b).wait()


def place(info, parts, shape):
    return pl.pallas_call(
        place_kernel,
        out_shape=jax.ShapeDtypeStruct(shape, bf16),
        in_specs=[SMEM] + [VMEM] * 4,
        out_specs=ANY,
        scratch_shapes=[pltpu.SemaphoreType.DMA((8,))],
        compiler_params=pltpu.CompilerParams(vmem_limit_bytes=4 * 1024 * 1024),
        cost_estimate=CHEAP,
    )(info, *parts)


def body(activations, cotangent, kv_weight, momentum, alive_mask):
    weight, mom = kv_weight[0], momentum[0]
    features, width = weight.shape
    scale = 1.0 / math.sqrt(features)
    t = lax.axis_index("tensor")
    core = lax.rem(lax.axis_index("dp"), 2)
    alive = alive_mask[0]
    chip = lax.rem(lax.axis_index("dp") // 2, GROUP // 2)
    info = jnp.stack([t ^ k for k in EARLY + LATE] + [core, chip, alive])

    a_y = tensor_swap(activations, 4)
    a_p = tensor_swap(activations, 1)
    a_q = tensor_swap(activations, 3)
    share = partials(scale, cotangent, weight)
    a_y, a_p, a_q, share = lax.optimization_barrier((a_y, a_p, a_q, share))

    a_yp = tensor_swap(a_p, 4)
    a_pq = tensor_swap(a_q, 1)
    a_qy = tensor_swap(a_y, 3)
    a_ypq = tensor_swap(after(activations, a_q), 6)
    *done, own_1 = update(
        scale,
        info,
        (activations, a_y, a_p, a_q),
        cotangent,
        weight,
        mom,
    )
    a_yp, a_pq, a_qy, a_ypq, share, *done = lax.optimization_barrier(
        (a_yp, a_pq, a_qy, a_ypq, share, *done)
    )
    new_momentum, keep, send, own_2 = update(
        scale, info, (a_yp, a_pq, a_qy, a_ypq), cotangent, weight, mom, done
    )

    members = lax.axis_size("tensor")
    share = after(share, send)
    shares = lax.all_to_all(
        share.reshape(members, share.shape[0] // members, features), "tensor", 0, 0, tiled=True
    )

    arrived = core_swap(send)
    sums = [(keep[k].astype(f32) + arrived[k].astype(f32)).astype(bf16) for k in range(4)]
    size = sums[0].shape[0] - PAD
    got = sums[0].astype(f32)
    for k in (2, 3, 1):
        got = got + chip_swap(sums[k], k).astype(f32)
    count = jnp.maximum(got[size : size + 1], 1.0)
    mean = (got[:size] / count).astype(bf16)
    input_grad = shares.astype(f32).sum(0).astype(bf16)
    mine = jnp.stack([after(mean, input_grad)] + [chip_swap(mean, k) for k in (1, 2, 3)])
    other = core_swap(mine)
    new_weight = place(info, (own_1, own_2, mine, other), weight.shape)
    return new_weight[None], new_momentum[None], input_grad


def solution(mesh):
    return jax.shard_map(
        body,
        mesh=mesh,
        in_specs=(
            P("dp", "tensor"),
            P("dp", "tensor"),
            P("dp", None, "tensor"),
            P("dp", None, "tensor"),
            P("dp"),
        ),
        out_specs=(P("dp", None, "tensor"), P("dp", None, "tensor"), P(("dp", "tensor"), None)),
        check_vma=False,
    )
```

```python
import functools
import math

import jax
import jax.numpy as jnp
from jax import lax
from jax.experimental import pallas as pl
from jax.experimental.pallas import tpu as pltpu
from jax.sharding import PartitionSpec as P

GROUP = 8
step_size = 0.25
decay_factor = 0.9
bf16 = jnp.bfloat16
f32 = jnp.float32

EARLY = (0, 4, 1, 3)
LATE = (5, 2, 7, 6)
PAD = 16
VMEM = pl.BlockSpec(memory_space=pltpu.VMEM)
ANY = pl.BlockSpec(memory_space=pl.ANY)
SMEM = pl.BlockSpec(memory_space=pltpu.SMEM)
PARAMS = pltpu.CompilerParams(vmem_limit_bytes=56 * 1024 * 1024)
CHEAP = pl.CostEstimate(flops=1000, bytes_accessed=1000, transcendentals=0)


def tensor_swap(value, k):
    return lax.ppermute(value, "tensor", [(t, t ^ k) for t in range(lax.axis_size("tensor"))])


def core_swap(value):
    return lax.ppermute(value, "dp", [(r, r ^ 1) for r in range(lax.axis_size("dp"))])


def chip_swap(value, k):
    return lax.ppermute(value, "dp", [(r, r ^ (2 * k)) for r in range(lax.axis_size("dp"))])


def after(value, *earlier):
    return lax.optimization_barrier((value, *earlier))[0]


def update_kernel(scale, first, info, *refs):
    n = 4
    base = 0 if first else n
    acts, (cot, weight, mom) = refs[:n], refs[n : n + 3]
    mom_out, keep, send, own = refs[n + 3 : n + 7] if first else refs[n + 6 : n + 10]
    a_buf, c_buf, w_buf, m_buf, o_buf, n_buf, p_buf, f_buf, sems = refs[-9:]
    size = w_buf.shape[1]
    width = w_buf.shape[2]
    core, chip, alive = info[8], info[9], info[10]

    def rows(b):
        return pl.ds(pl.multiple_of(info[base + b] * size, size), size)

    def loads(b):
        return (
            pltpu.make_async_copy(acts[b], a_buf.at[b], sems.at[0, b]),
            pltpu.make_async_copy(weight.at[rows(b)], w_buf.at[b], sems.at[1, b]),
            pltpu.make_async_copy(mom.at[rows(b)], m_buf.at[b], sems.at[2, b]),
        )

    def stores(b):
        return (
            pltpu.make_async_copy(o_buf.at[b], mom_out.at[rows(b)], sems.at[3, b]),
            pltpu.make_async_copy(n_buf.at[b], own.at[b], sems.at[4, b]),
        )

    def hand_over(b, target):
        place = (b % 2 + (0 if first else 2)) ^ chip
        return pltpu.make_async_copy(
            p_buf.at[b], target.at[place, pl.ds(0, size)], sems.at[5, b]
        )

    def flags(k):
        return tuple(
            pltpu.make_async_copy(f_buf, target.at[k, pl.ds(size, PAD)], sems.at[6 + i, k])
            for i, target in enumerate((keep, send))
        )

    load_cot = pltpu.make_async_copy(cot, c_buf, sems.at[8, 0])
    load_cot.start()
    for b in range(n):
        for copy in loads(b):
            copy.start()
    flag = jnp.where(alive > 0, 1.0, 0.0).astype(f32)
    if first:
        f_buf[...] = jnp.full((PAD, width), flag, f32).astype(bf16)
        for k in range(4):
            for copy in flags(k):
                copy.start()
    load_cot.wait()
    for b in range(n):
        for copy in loads(b):
            copy.wait()
        grad = lax.dot_general(
            a_buf[b], c_buf[...], (((0,), (0,)), ((), ())), preferred_element_type=f32
        )
        moment = decay_factor * m_buf[b].astype(f32) + grad * scale
        o_buf[b] = moment.astype(bf16)
        new = w_buf[b].astype(f32) - step_size * moment
        n_buf[b] = new.astype(bf16)
        p_buf[b] = (new * flag).astype(bf16)
        for copy in stores(b):
            copy.start()

        @pl.when(core == b // 2)
        def _():
            hand_over(b, keep).start()

        @pl.when(core != b // 2)
        def _():
            hand_over(b, send).start()

    for b in range(n):
        for copy in stores(b):
            copy.wait()
        hand_over(b, keep).wait()
    if first:
        for k in range(4):
            for copy in flags(k):
                copy.wait()


def update(scale, info, acts, cot, weight, mom, done=()):
    first = not done
    rows, size = acts[0].shape
    width = cot.shape[1]
    block = pltpu.VMEM((4, size, width), bf16)
    return pl.pallas_call(
        functools.partial(update_kernel, scale, first),
        out_shape=(
            jax.ShapeDtypeStruct(weight.shape, bf16),
            jax.ShapeDtypeStruct((4, size + PAD, width), bf16),
            jax.ShapeDtypeStruct((4, size + PAD, width), bf16),
            jax.ShapeDtypeStruct((4, size, width), bf16),
        ),
        in_specs=[SMEM] + [ANY] * (7 + len(done)),
        out_specs=(ANY, ANY, ANY, ANY),
        scratch_shapes=[
            pltpu.VMEM((4, rows, size), bf16),
            pltpu.VMEM((rows, width), bf16),
            block,
            block,
            block,
            block,
            block,
            pltpu.VMEM((PAD, width), bf16),
            pltpu.SemaphoreType.DMA((9, 4)),
        ],
        input_output_aliases={} if first else {8: 0, 9: 1, 10: 2},
        compiler_params=PARAMS,
        cost_estimate=CHEAP,
    )(info, *acts, cot, weight, mom, *done)


def partial_kernel(scale, cot, weight, out, c_buf, w_buf, buf, sems):
    tiles = 4
    size = weight.shape[0] // tiles

    def load(n):
        at = pl.ds(n * size, size)
        return pltpu.make_async_copy(weight.at[at], w_buf.at[at], sems.at[n])

    def store(n):
        return pltpu.make_async_copy(buf.at[n], out.at[:, pl.ds(n * size, size)], sems.at[tiles + n])

    load_cot = pltpu.make_async_copy(cot, c_buf, sems.at[2 * tiles])
    load_cot.start()
    for n in range(tiles):
        load(n).start()
    load_cot.wait()
    for n in range(tiles):
        load(n).wait()
        value = lax.dot_general(
            c_buf[...],
            w_buf[n * size : (n + 1) * size, :],
            (((1,), (1,)), ((), ())),
            preferred_element_type=f32,
        )
        buf[n] = (value * scale).astype(bf16)
        store(n).start()
    for n in range(tiles):
        store(n).wait()


def partials(scale, cot, weight):
    rows, features = cot.shape[0], weight.shape[0]
    return pl.pallas_call(
        functools.partial(partial_kernel, scale),
        out_shape=jax.ShapeDtypeStruct((rows, features), bf16),
        in_specs=[ANY, ANY],
        out_specs=ANY,
        scratch_shapes=[
            pltpu.VMEM(cot.shape, bf16),
            pltpu.VMEM(weight.shape, bf16),
            pltpu.VMEM((4, rows, features // 4), bf16),
            pltpu.SemaphoreType.DMA((9,)),
        ],
        compiler_params=PARAMS,
        cost_estimate=CHEAP,
    )(cot, weight)


def place_kernel(info, own_1, own_2, mine, other, out, sems):
    size = mine.shape[1]
    core, chip, alive = info[8], info[9], info[10]

    def copy(source, b):
        at = pl.ds(pl.multiple_of(info[b] * size, size), size)
        return pltpu.make_async_copy(source, out.at[at], sems.at[b])

    for b in range(8):
        own = own_1 if b < 4 else own_2
        slot = (b % 2 + 2 * (b // 4)) ^ chip
        is_mine = core == (b % 4) // 2

        @pl.when(alive <= 0)
        def _():
            copy(own.at[b % 4], b).start()

        @pl.when((alive > 0) & is_mine)
        def _():
            copy(mine.at[slot], b).start()

        @pl.when((alive > 0) & jnp.logical_not(is_mine))
        def _():
            copy(other.at[slot], b).start()

    for b in range(8):
        copy(mine.at[0], b).wait()


def place(info, parts, shape):
    return pl.pallas_call(
        place_kernel,
        out_shape=jax.ShapeDtypeStruct(shape, bf16),
        in_specs=[SMEM] + [VMEM] * 4,
        out_specs=ANY,
        scratch_shapes=[pltpu.SemaphoreType.DMA((8,))],
        compiler_params=pltpu.CompilerParams(vmem_limit_bytes=4 * 1024 * 1024),
        cost_estimate=CHEAP,
    )(info, *parts)


def body(activations, cotangent, kv_weight, momentum, alive_mask):
    weight, mom = kv_weight[0], momentum[0]
    features, width = weight.shape
    scale = 1.0 / math.sqrt(features)
    t = lax.axis_index("tensor")
    core = lax.rem(lax.axis_index("dp"), 2)
    alive = alive_mask[0]
    chip = lax.rem(lax.axis_index("dp") // 2, GROUP // 2)
    info = jnp.stack([t ^ k for k in EARLY + LATE] + [core, chip, alive])

    a_y = tensor_swap(activations, 4)
    a_p = tensor_swap(activations, 1)
    a_q = tensor_swap(activations, 3)
    share = partials(scale, cotangent, weight)
    a_y, a_p, a_q, share, info = lax.optimization_barrier((a_y, a_p, a_q, share, info))

    a_yp = tensor_swap(a_p, 4)
    a_pq = tensor_swap(a_q, 1)
    a_qy = tensor_swap(a_y, 3)
    a_ypq = tensor_swap(after(activations, a_q), 6)
    *done, own_1 = update(
        scale,
        info,
        (activations, a_y, a_p, a_q),
        cotangent,
        weight,
        mom,
    )
    a_yp, a_pq, a_qy, a_ypq, share, *done = lax.optimization_barrier(
        (a_yp, a_pq, a_qy, a_ypq, share, *done)
    )
    new_momentum, keep, send, own_2 = update(
        scale, info, (a_yp, a_pq, a_qy, a_ypq), cotangent, weight, mom, done
    )

    members = lax.axis_size("tensor")
    share = after(share, send)
    shares = lax.all_to_all(
        share.reshape(members, share.shape[0] // members, features), "tensor", 0, 0, tiled=True
    )

    arrived = core_swap(send)
    sums = [(keep[k].astype(f32) + arrived[k].astype(f32)).astype(bf16) for k in range(4)]
    size = sums[0].shape[0] - PAD
    got = sums[0].astype(f32)
    for k in (2, 3, 1):
        got = got + chip_swap(sums[k], k).astype(f32)
    count = jnp.maximum(got[size : size + 1], 1.0)
    mean = (got[:size] / count).astype(bf16)
    input_grad = shares.astype(f32).sum(0).astype(bf16)
    mine = jnp.stack([after(mean, input_grad)] + [chip_swap(mean, k) for k in (1, 2, 3)])
    other = core_swap(mine)
    new_weight = place(info, (own_1, own_2, mine, other), weight.shape)
    return new_weight[None], new_momentum[None], input_grad


def solution(mesh):
    return jax.shard_map(
        body,
        mesh=mesh,
        in_specs=(
            P("dp", "tensor"),
            P("dp", "tensor"),
            P("dp", None, "tensor"),
            P("dp", None, "tensor"),
            P("dp"),
        ),
        out_specs=(P("dp", None, "tensor"), P("dp", None, "tensor"), P(("dp", "tensor"), None)),
        check_vma=False,
    )
```
